512 devices in a mesh: mode: 8 (over y_hi, core), pen: 64 (over y_lo, z, x).
Axes of the slice: x: 4, y: 8 (y_hi: 4, y_lo: 2; y = y_hi * 2 + y_lo), z: 8, core: 2. Of those that a mesh axis runs over, the one named last changes fastest.
Arguments:
- object_field: bfloat16 [2, 256, 256, 256], P(None, 'pen'), may hold values from -6 to 6
- probes: bfloat16 [8, 2, 256, 256, 256], P('mode', None, 'pen'), may hold values from -3 to 3
- measured: float32 [256, 256, 256], P(None, 'pen'), may hold values from 8 to 128
Outputs:
- gradient: float32 [2, 256, 256, 256], P(None, 'pen', 'mode')
The draws below stay inside these ranges and needn't reach their ends.
All inputs are finite; a program needn't handle non-finite values.
Results may differ from the reference program's by a relative error of at most 0.0003.
Values sent between devices are 32-bit elements; how exact they have to be, the bound alone decides.
A program may use at most 64 MiB of HBM per device.

```python
import math
import jax
import jax.numpy as jnp
from jax import lax

N = 256
MODES = 8


def steps_of(rng, shape, pieces, least, largest):
    level, own = 1.0, jax.random.fold_in(rng, 6)
    for dim, shards_of in pieces:
        draws = jnp.exp(jax.random.uniform(jax.random.fold_in(own, dim), (shards_of,), jnp.float32, least / len(pieces), largest / len(pieces)))
        level = level * jnp.repeat(draws, shape[dim] // shards_of).reshape([-1 if axis == dim else 1 for axis in range(len(shape))])
    return level


def scatter_about(own_key, shape, deviation, most, pieces=(), kind=jnp.bfloat16):
    factor_of = steps_of(own_key, shape, pieces, -0.22, 0.18) if pieces else 1.0
    entries = jax.random.normal(own_key, shape, jnp.float32) * deviation * factor_of
    return jnp.minimum(jnp.maximum(entries, -most), most).astype(kind)


def setup_inputs(seed: int = 0) -> dict:
    keys = jax.random.split(jax.random.key(seed), 4)
    return {
        "object_field": scatter_about(keys[0], (2, N, N, N), 1.0, 6.0, ((1, 64),)),
        "probes": scatter_about(keys[1], (MODES, 2, N, N, N), 0.5, 3.0, ((0, 8), (2, 64))),
        "measured": jnp.clip(jnp.exp(math.log(128.0) - 2.7725887 * jax.random.uniform(keys[2], (N, N, N), jnp.float32) ** steps_of(keys[2], (N, N, N), ((1, 64),), -0.2, 0.2)), 8.0, 128.0),
    }


def reference(object_field, probes, measured):
    obj = lax.complex(object_field[0].astype(jnp.float32), object_field[1].astype(jnp.float32))
    total = jnp.zeros(measured.shape, jnp.float32)
    for mode in range(MODES):
        probe = lax.complex(probes[mode, 0].astype(jnp.float32), probes[mode, 1].astype(jnp.float32))
        spectrum = jnp.fft.fftn(probe * obj, norm='ortho')
        total = total + jnp.real(spectrum * jnp.conj(spectrum))
    ratio = jnp.sqrt(measured) / jnp.sqrt(total + 0.1)
    accum = jnp.zeros(obj.shape, obj.dtype)
    for mode in range(MODES):
        probe = lax.complex(probes[mode, 0].astype(jnp.float32), probes[mode, 1].astype(jnp.float32))
        exit_wave = probe * obj
        revised = jnp.fft.ifftn(ratio * jnp.fft.fftn(exit_wave, norm='ortho'), norm='ortho')
        accum = accum + jnp.conj(probe) * (revised - exit_wave)
    return jnp.stack([jnp.real(accum), jnp.imag(accum)])
```

```python
import functools
import math

import jax
import jax.numpy as jnp
import ml_dtypes
import numpy as np
from jax import lax
from jax.experimental import pallas as pl
from jax.experimental.pallas import tpu as pltpu
from jax.sharding import PartitionSpec as P

DAMP = 0.1
N = 256
H = N // 2
F32 = jnp.float32
BF16 = jnp.bfloat16
MESH = pl.DeviceIdType.MESH


def forward_matrix(parity):
    freq = 2 * np.arange(H) + parity
    angle = 2.0 * math.pi / N * ((freq[:, None] * np.arange(H)[None, :]) % N)
    cosine, sine = np.cos(angle) / math.sqrt(N), np.sin(angle) / math.sqrt(N)
    return np.block([[cosine, sine], [-sine, cosine]])


def inverse_matrix(parity):
    return forward_matrix(parity).T


def split(matrix):
    high = matrix.astype(ml_dtypes.bfloat16)
    low = (matrix - high.astype(np.float64)).astype(ml_dtypes.bfloat16)
    return np.stack([high, low])


def tables():
    slab, part, row = np.meshgrid(np.arange(H // 4), np.arange(2), np.arange(4), indexing="ij")
    order = (part * H + slab * 4 + row).reshape(-1)
    sets = []
    for parity in range(2):
        fwd, inv = forward_matrix(parity), inverse_matrix(parity)
        sets.append(
            [split(fwd.T), split(fwd), split(fwd[:, order]), split(inv[order, :]), split(inv), split(inv.T)]
        )
    weights = np.stack([np.stack([sets[0][k], sets[1][k]]) for k in range(6)])
    rows = np.zeros((N, N), np.float32)
    rows[np.arange(N), np.concatenate([np.arange(0, N, 2), np.arange(1, N, 2)])] = 1.0
    return weights, rows


def halves(value):
    high = value.astype(BF16)
    return high, (value - high.astype(F32)).astype(BF16)


def dot(left, right):
    return jnp.dot(left, right, preferred_element_type=F32)


def table_first(table, value):
    high, low = halves(value)
    return dot(table[0], high) + (dot(table[0], low) + dot(table[1], high))


def table_last(value, table):
    high, low = halves(value)
    return dot(high, table[0]) + (dot(low, table[0]) + dot(high, table[1]))


def place():
    mode, pen = lax.axis_index("mode"), lax.axis_index("pen")
    return dict(mode=mode, pen=pen, y_hi=mode // 2, core=mode % 2, y=pen // 32, z=(pen // 4) % 8, x=pen % 4)


def pen_at(me, step):
    t = (step * 29) % 64
    x, y, z = (me["x"] + t % 4) % 4, (me["y"] + (t // 4) % 2) % 2, (me["z"] + t // 8) % 8
    return y * 32 + z * 4 + x


def signal(device):
    pl.semaphore_signal(pltpu.get_barrier_semaphore(), inc=1, device_id=device, device_id_type=MESH)


def greet_pens(me):
    @pl.loop(1, 64)
    def _(step):
        signal({"pen": pen_at(me, step)})


def greet_modes(me):
    for step in range(1, 8):
        signal({"mode": (me["mode"] + step) % 8})


def await_greetings(count):
    pl.semaphore_wait(pltpu.get_barrier_semaphore(), count)


def ship(source, target, ssem, rsem, device):
    return pltpu.make_async_remote_copy(
        src_ref=source, dst_ref=target, send_sem=ssem, recv_sem=rsem, device_id=device, device_id_type=MESH
    )


def wait_bytes(ref, sem):
    pltpu.make_async_copy(ref, ref, sem).wait()


def exit_wave(obj, prb, x):
    p_re, p_im = prb[0, x].astype(F32), prb[1, x].astype(F32)
    o_re, o_im = obj[0, x].astype(F32), obj[1, x].astype(F32)
    return p_re, p_im, p_re * o_re - p_im * o_im, p_re * o_im + p_im * o_re


def send_pens(me, source, target, half, send_sem, recv_sem):
    @pl.loop(1, 64)
    def _(step):
        pen = pen_at(me, step)
        ship(
            source.at[half, pen], target.at[half, me["pen"]], send_sem.at[half], recv_sem.at[half], {"pen": pen}
        ).start()


def outward(obj, prb, wz, wy, recv, send, send_sem, recv_sem, own_sem):
    me = place()
    greet_pens(me)
    for half in range(2):
        for two in range(2):
            lines = []
            for x in (2 * two, 2 * two + 1):
                _, _, e_re, e_im = exit_wave(obj, prb, x)
                if half == 0:
                    mixed = jnp.concatenate([e_re[:, :H] + e_re[:, H:], e_im[:, :H] + e_im[:, H:]], axis=1)
                else:
                    mixed = jnp.concatenate([e_re[:, :H] - e_re[:, H:], e_im[:, :H] - e_im[:, H:]], axis=1)
                lines.append(table_last(mixed, wz[half]))
            re = jnp.concatenate([lines[0][:, :H], lines[1][:, :H]], axis=1)
            im = jnp.concatenate([lines[0][:, H:], lines[1][:, H:]], axis=1)
            for parity in range(2):
                if parity == 0:
                    mixed = jnp.concatenate([re[:H] + re[H:], im[:H] + im[H:]], axis=0)
                else:
                    mixed = jnp.concatenate([re[:H] - re[H:], im[:H] - im[H:]], axis=0)
                result = table_first(wy[parity], mixed)
                for c in range(2):
                    for k in range(2):
                        rows = pl.ds(parity * 8 + c * 4 + 2 * two + k, H, stride=16)
                        flat = send.at[half].reshape(N * 8, H)
                        flat[rows, :] = result[c * H : (c + 1) * H, k * H : (k + 1) * H]
        if half == 0:
            await_greetings(63)
        send_pens(me, send, recv, half, send_sem, recv_sem)
    own = [
        pltpu.make_async_copy(send.at[half, me["pen"]], recv.at[half, me["pen"]], own_sem.at[half])
        for half in range(2)
    ]
    for half in range(2):
        own[half].start()
    for half in range(2):
        own[half].wait()
        wait_bytes(send.at[half, pl.ds(0, 63)], recv_sem.at[half])
        wait_bytes(send.at[half, pl.ds(0, 63)], send_sem.at[half])


def middle(
    recv, meas, wx, vx, perm, back, spec, power, pair, sums, near, ratio,
    pair_send, pair_recv, near_send, near_recv, all_send, all_recv, sib_send, sib_recv,
):
    me = place()
    core, other, y_hi = me["core"], 1 - me["core"], me["y_hi"]
    greet_modes(me)
    sibling = {"mode": y_hi * 2 + other}

    def group(d):
        return (y_hi + d) % 4

    def chip(d):
        return {"mode": group(d) * 2 + core}

    def to_pair(d):
        return ship(power.at[d, other], pair.at[d], pair_send.at[d], pair_recv.at[d], sibling)

    def to_near(d):
        return ship(sums.at[d], near.at[d - 1], near_send.at[d - 1], near_recv.at[d - 1], chip(d))

    def to_all(d):
        return ship(ratio.at[0, core], ratio.at[4 - d, core], all_send.at[d - 1], all_recv.at[d - 1], chip(d))

    def to_sibling(d):
        return ship(ratio.at[d, core], ratio.at[d, core], sib_send.at[d], sib_recv.at[d], sibling)

    def from_sibling(d):
        return ship(ratio.at[d, other], ratio.at[d, other], sib_send.at[d], sib_recv.at[d], sibling)

    far_first = (2, 1, 3, 0)

    def hand_on(d):
        to_pair(d).wait_recv()
        sums[d] = power[d, core] + pair[d]
        if d:
            to_near(d).start()

    last = None
    for d in far_first:
        rows = pl.ds(pl.multiple_of(group(d) * 8, 8), 8)
        value = jnp.concatenate([recv[h, :, rows, :].reshape(2 * N, H) for h in range(2)], axis=1)
        top, bottom = value[:N], value[N:]
        for parity in range(2):
            result = table_first(wx[parity], top + bottom if parity == 0 else top - bottom)
            spec[d, parity] = result
            square = result * result
            square = square[:H] + square[H:]
            for h in range(2):
                power[d, h, parity * H : (parity + 1) * H, :] = square[:, h * H : (h + 1) * H]
        if last is None:
            await_greetings(7)
        to_pair(d).start()
        if last is not None:
            hand_on(last)
        last = d
    hand_on(last)

    own = meas[:, pl.ds(y_hi, 1), :].reshape(N, N)
    root = jnp.dot(perm[...], jnp.sqrt(own), precision=lax.Precision.HIGHEST, preferred_element_type=F32)
    root = lax.dot_general(
        root, perm[pl.ds(pl.multiple_of(core * H, H), H), :], (((1,), (1,)), ((), ())),
        precision=lax.Precision.HIGHEST, preferred_element_type=F32,
    )

    for d in range(1, 4):
        to_near(d).wait_recv()
    total = (sums[0] + near[0]) + (near[1] + near[2])
    ratio[0, core] = root / jnp.sqrt(total + DAMP)
    for d in (2, 1, 3):
        to_all(d).start()
    to_sibling(0).start()

    def finish(d):
        from_sibling(d).wait_recv()
        parts = []
        for parity in range(2):
            half = slice(parity * H, (parity + 1) * H)
            scale = jnp.concatenate([ratio[d, 0, half], ratio[d, 1, half]], axis=1)
            scale = jnp.concatenate([scale, scale], axis=0)
            parts.append(table_first(vx[parity], spec[d, parity] * scale))
        rows = pl.ds(pl.multiple_of(group(d) * 8, 8), 8)
        for side in range(2):
            result = parts[0] + parts[1] if side == 0 else parts[0] - parts[1]
            for h in range(2):
                back[h, side * 32 : (side + 1) * 32, rows, :] = result[:, h * H : (h + 1) * H].reshape(32, 8, H)

    finish(0)
    order = (1, 3, 2)
    for place_in, d in enumerate(order):
        to_all(4 - d).wait_recv()
        to_sibling(d).start()
        if place_in:
            finish(order[place_in - 1])
    finish(order[-1])

    for d in range(4):
        to_pair(d).wait_send()
        to_sibling(d).wait_send()
        if d:
            to_near(d).wait_send()
            to_all(d).wait_send()


def homeward(back, ret, send_sem, recv_sem, own_sem):
    me = place()
    greet_pens(me)
    own = [
        pltpu.make_async_copy(back.at[half, me["pen"]], ret.at[half, me["pen"]], own_sem.at[half])
        for half in range(2)
    ]
    for half in range(2):
        own[half].start()
    await_greetings(63)
    for half in range(2):
        send_pens(me, back, ret, half, send_sem, recv_sem)
    for half in range(2):
        own[half].wait()
        wait_bytes(back.at[half, pl.ds(0, 63)], recv_sem.at[half])
        wait_bytes(back.at[half, pl.ds(0, 63)], send_sem.at[half])


def update(
    obj, prb, ret, vy, vz, out, part, pair, total, near, pair_send, pair_recv, near_send, near_recv
):
    me = place()
    core, other, y_hi = me["core"], 1 - me["core"], me["y_hi"]
    greet_modes(me)

    def to_core(x):
        return ship(
            part.at[other, x], pair.at[x], pair_send.at[x], pair_recv.at[x], {"mode": y_hi * 2 + other}
        )

    def to_chip(x, d):
        target = (y_hi + d) % 4
        return ship(
            total.at[x, target], near.at[x, d - 1], near_send.at[x, d - 1], near_recv.at[x, d - 1],
            {"mode": target * 2 + core},
        )

    def forward(x):
        to_core(x).wait_recv()
        total[x] = part[core, x] + pair[x]
        for d in (2, 1, 3):
            to_chip(x, d).start()

    for two in range(2):
        columns = []
        for half in range(2):
            flat = ret.at[half].reshape(N * 8, H)
            pieces = []
            for parity in range(2):
                blocks = [
                    [flat[pl.ds(parity * 8 + c * 4 + 2 * two + k, H, stride=16), :] for k in range(2)]
                    for c in range(2)
                ]
                value = jnp.concatenate([jnp.concatenate(b, axis=1) for b in blocks], axis=0)
                pieces.append(table_first(vy[parity], value))
            columns.append((pieces[0] + pieces[1], pieces[0] - pieces[1]))
        for k in range(2):
            x = 2 * two + k
            lanes = slice(k * H, (k + 1) * H)
            lines = []
            for half in range(2):
                top, bottom = columns[half]
                re = jnp.concatenate([top[:H, lanes], bottom[:H, lanes]], axis=0)
                im = jnp.concatenate([top[H:, lanes], bottom[H:, lanes]], axis=0)
                lines.append(table_last(jnp.concatenate([re, im], axis=1), vz[half]))
            low, high = lines[0] + lines[1], lines[0] - lines[1]
            p_re, p_im, e_re, e_im = exit_wave(obj, prb, x)
            d_re = jnp.concatenate([low[:, :H], high[:, :H]], axis=1) - e_re
            d_im = jnp.concatenate([low[:, H:], high[:, H:]], axis=1) - e_im
            g_re = p_re * d_re + p_im * d_im
            g_im = p_re * d_im - p_im * d_re
            for chunk in range(8):
                rows = slice(32 * chunk, 32 * chunk + 32)
                part[chunk % 2, x, chunk // 2, 0] = g_re[rows]
                part[chunk % 2, x, chunk // 2, 1] = g_im[rows]
            if x == 0:
                await_greetings(7)
            to_core(x).start()
            if x > 0:
                forward(x - 1)
    forward(3)
    for x in range(4):
        for d in range(1, 4):
            to_chip(x, d).wait_recv()
        out[:, x] = (total[x, y_hi] + near[x, 0]) + (near[x, 1] + near[x, 2])
    for x in range(4):
        to_core(x).wait_send()
        for d in range(1, 4):
            to_chip(x, d).wait_send()


def call(body, name, number, inputs, result, result_space, scratch, arrays):
    return pl.pallas_call(
        body,
        out_shape=jax.ShapeDtypeStruct(result, F32),
        in_specs=[pl.BlockSpec(memory_space=space) for space in inputs],
        out_specs=pl.BlockSpec(memory_space=result_space),
        scratch_shapes=scratch,
        compiler_params=pltpu.CompilerParams(
            collective_id=number, has_side_effects=True, vmem_limit_bytes=40 * 2**20
        ),
        name=name,
    )(*arrays)


def shards(object_field, probes, measured):
    weights, rows = tables()
    wz, wy, wx, vx, vy, vz = [jnp.asarray(weights[k]) for k in range(6)]
    vmem, anywhere = pltpu.VMEM, pl.ANY
    dma = pltpu.SemaphoreType.DMA
    slab = (2, 64, 32, H)
    prb = probes[0]
    recv = call(
        outward, "outward", 0, [vmem] * 4, slab, anywhere,
        [vmem(slab, F32), dma((2,)), dma((2,)), dma((2,))],
        (object_field, prb, wz, wy),
    )
    back = call(
        middle, "middle", 1, [vmem] * 5, slab, vmem,
        [
            vmem((4, 2, N, N), F32),
            vmem((4, 2, N, H), F32),
            vmem((4, N, H), F32),
            vmem((4, N, H), F32),
            vmem((3, N, H), F32),
            vmem((4, 2, N, H), F32),
            dma((4,)), dma((4,)), dma((3,)), dma((3,)), dma((3,)), dma((3,)), dma((4,)), dma((4,)),
        ],
        (recv, measured, wx, vx, jnp.asarray(rows)),
    )
    ret = call(
        homeward, "homeward", 2, [anywhere], slab, anywhere, [dma((2,)), dma((2,)), dma((2,))], (back,)
    )
    return call(
        update, "update", 3, [vmem] * 5, (2, 4, 32, N), vmem,
        [
            vmem((2, 4, 4, 2, 32, N), F32),
            vmem((4, 4, 2, 32, N), F32),
            vmem((4, 4, 2, 32, N), F32),
            vmem((4, 3, 2, 32, N), F32),
            dma((4,)), dma((4,)), dma((4, 3)), dma((4, 3)),
        ],
        (object_field, prb, ret, vy, vz),
    )


def solution(mesh):
    return jax.shard_map(
        shards,
        mesh=mesh,
        in_specs=(
            P(None, "pen", None, None),
            P("mode", None, "pen", None, None),
            P(None, "pen", None),
        ),
        out_specs=P(None, "pen", "mode", None),
        check_vma=False,
    )
```

```python
import functools
import math

import jax
import jax.numpy as jnp
import ml_dtypes
import numpy as np
from jax import lax
from jax.experimental import pallas as pl
from jax.experimental.pallas import tpu as pltpu
from jax.sharding import PartitionSpec as P

DAMP = 0.1
N = 256
H = N // 2
F32 = jnp.float32
BF16 = jnp.bfloat16
MESH = pl.DeviceIdType.MESH


def forward_matrix(parity):
    freq = 2 * np.arange(H) + parity
    angle = 2.0 * math.pi / N * ((freq[:, None] * np.arange(H)[None, :]) % N)
    cosine, sine = np.cos(angle) / math.sqrt(N), np.sin(angle) / math.sqrt(N)
    return np.block([[cosine, sine], [-sine, cosine]])


def inverse_matrix(parity):
    return forward_matrix(parity).T


def split(matrix):
    high = matrix.astype(ml_dtypes.bfloat16)
    low = (matrix - high.astype(np.float64)).astype(ml_dtypes.bfloat16)
    return np.stack([high, low])


def tables():
    slab, part, row = np.meshgrid(np.arange(H // 4), np.arange(2), np.arange(4), indexing="ij")
    order = (part * H + slab * 4 + row).reshape(-1)
    sets = []
    for parity in range(2):
        fwd, inv = forward_matrix(parity), inverse_matrix(parity)
        sets.append(
            [split(fwd.T), split(fwd), split(fwd[:, order]), split(inv[order, :]), split(inv), split(inv.T)]
        )
    weights = np.stack([np.stack([sets[0][k], sets[1][k]]) for k in range(6)])
    rows = np.zeros((N, N), np.float32)
    rows[np.arange(N), np.concatenate([np.arange(0, N, 2), np.arange(1, N, 2)])] = 1.0
    return weights, rows


def halves(value):
    high = value.astype(BF16)
    return high, (value - high.astype(F32)).astype(BF16)


def dot(left, right):
    return jnp.dot(left, right, preferred_element_type=F32)


def table_first(table, value):
    high, low = halves(value)
    return dot(table[0], high) + (dot(table[0], low) + dot(table[1], high))


def table_last(value, table):
    high, low = halves(value)
    return dot(high, table[0]) + (dot(low, table[0]) + dot(high, table[1]))


def place():
    mode, pen = lax.axis_index("mode"), lax.axis_index("pen")
    return dict(
        mode=mode, pen=pen, y_hi=mode // 2, core=mode % 2, y=(mode // 2) * 2 + pen // 32, z=(pen // 4) % 8, x=pen % 4
    )


def chip_at(me, step):
    t = (step * 181) % 256
    x, y, z = (me["x"] + t % 4) % 4, (me["y"] + (t // 4) % 8) % 8, (me["z"] + t // 32) % 8
    return y // 2, (y % 2) * 32 + z * 4 + x


def z_peer(me, step):
    return {"pen": me["pen"] // 32 * 32 + (me["z"] + step) % 8 * 4 + me["x"]}


def xy_peer(me, step):
    other = (me["pen"] // 32 * 4 + me["x"] + step) % 8
    return {"pen": other // 4 * 32 + me["z"] * 4 + other % 4}


def mode_peer(me, step):
    return {"mode": (me["mode"] + step) % 8}


def greet(semaphore, me, *kinds):
    for kind in kinds:
        for step in range(1, 8):
            pl.semaphore_signal(semaphore, inc=1, device_id=kind(me, step), device_id_type=MESH)


def meet_all(me, lines, planes):
    barrier = pltpu.get_barrier_semaphore()
    greet(barrier, me, mode_peer, z_peer, xy_peer)
    pl.semaphore_wait(barrier, 21)
    greet(lines, me, z_peer)
    pl.semaphore_wait(lines, 7)
    greet(planes, me, xy_peer)
    pl.semaphore_wait(planes, 7)


def ship(source, target, ssem, rsem, device):
    return pltpu.make_async_remote_copy(
        src_ref=source, dst_ref=target, send_sem=ssem, recv_sem=rsem, device_id=device, device_id_type=MESH
    )


def wait_bytes(ref, sem):
    pltpu.make_async_copy(ref, ref, sem).wait()


def exit_wave(obj, prb, x):
    p_re, p_im = prb[0, x].astype(F32), prb[1, x].astype(F32)
    o_re, o_im = obj[0, x].astype(F32), obj[1, x].astype(F32)
    return p_re, p_im, p_re * o_re - p_im * o_im, p_re * o_im + p_im * o_re


def transform_zy(obj, prb, meas, wz, wy, perm, send, root):
    me = place()
    own = meas[:, pl.ds(me["y_hi"], 1), :].reshape(N, N)
    rows = jnp.dot(perm[...], jnp.sqrt(own), precision=lax.Precision.HIGHEST, preferred_element_type=F32)
    root[...] = lax.dot_general(
        rows, perm[pl.ds(pl.multiple_of(me["core"] * H, H), H), :], (((1,), (1,)), ((), ())),
        precision=lax.Precision.HIGHEST, preferred_element_type=F32,
    )
    for half in range(2):
        for two in range(2):
            lines = []
            for x in (2 * two, 2 * two + 1):
                _, _, e_re, e_im = exit_wave(obj, prb, x)
                if half == 0:
                    mixed = jnp.concatenate([e_re[:, :H] + e_re[:, H:], e_im[:, :H] + e_im[:, H:]], axis=1)
                else:
                    mixed = jnp.concatenate([e_re[:, :H] - e_re[:, H:], e_im[:, :H] - e_im[:, H:]], axis=1)
                lines.append(table_last(mixed, wz[half]))
            re = jnp.concatenate([lines[0][:, :H], lines[1][:, :H]], axis=1)
            im = jnp.concatenate([lines[0][:, H:], lines[1][:, H:]], axis=1)
            for parity in range(2):
                if parity == 0:
                    mixed = jnp.concatenate([re[:H] + re[H:], im[:H] + im[H:]], axis=0)
                else:
                    mixed = jnp.concatenate([re[:H] - re[H:], im[:H] - im[H:]], axis=0)
                result = table_first(wy[parity], mixed)
                flat = send.at[pl.ds(half * N, N)].reshape(N * 8, H)
                for c in range(2):
                    for k in range(2):
                        rows = pl.ds(parity * 8 + c * 4 + 2 * two + k, H, stride=16)
                        flat[rows, :] = result[c * H : (c + 1) * H, k * H : (k + 1) * H]


def send_half(me, half, source, target, send_sem, recv_sem):
    @pl.loop(1, 256)
    def _(step):
        y_hi, pen = chip_at(me, step)
        mode = y_hi * 2 + half
        ship(source(mode, pen), target, send_sem, recv_sem, {"mode": mode, "pen": pen}).start()


def send_home(me, source, target, send_sem, recv_sem, own_sem):
    sibling = me["y_hi"] * 2 + 1 - me["core"]
    ship(source(sibling, me["pen"]), target, send_sem, recv_sem, {"mode": sibling}).start()
    own = pltpu.make_async_copy(source(me["mode"], me["pen"]), target, own_sem)
    own.start()
    own.wait()


def exchange(
    send, root, wx, vx, ret, recv, lines, planes, send_sem, recv_sem, back_sem, ret_sem, own_sem
):
    me = place()
    meet_all(me, lines, planes)

    def tile(mode, pen):
        return send.at[mode % 2 * N + 4 * pen + mode // 2]

    landing = recv.at[me["mode"] * 64 + me["pen"]]
    for half in range(2):
        send_half(me, half, tile, landing, send_sem, recv_sem)
    send_home(me, tile, landing, send_sem, recv_sem, own_sem)
    wait_bytes(recv.at[pl.ds(0, 511)], recv_sem)

    def slab(mode):
        return recv.at[pl.ds(64 * mode, 64)].reshape(2 * N, H)

    power = [jnp.zeros((H, H), F32), jnp.zeros((H, H), F32)]
    for two in range(4):
        value = jnp.concatenate([slab(2 * two + k)[...] for k in range(2)], axis=1)
        top, bottom = value[:N], value[N:]
        for parity in range(2):
            result = table_first(wx[parity], top + bottom if parity == 0 else top - bottom)
            for k in range(2):
                slab(2 * two + k)[parity * N : (parity + 1) * N, :] = result[:, k * H : (k + 1) * H]
            square = result * result
            square = square[:H] + square[H:]
            power[parity] = power[parity] + (square[:, :H] + square[:, H:])
    ratio = [root[parity * H : (parity + 1) * H] / jnp.sqrt(power[parity] + DAMP) for parity in range(2)]
    ratio = [jnp.concatenate([r, r], axis=0) for r in ratio]
    ratio = [jnp.concatenate([r, r], axis=1) for r in ratio]

    def home(mode, pen):
        return recv.at[mode * 64 + pen]

    target = ret.at[me["core"] * N + 4 * me["pen"] + me["y_hi"]]
    for half in range(2):
        for two in range(2):
            modes = (4 * two + half, 4 * two + 2 + half)
            parts = []
            for parity in range(2):
                rows = slice(parity * N, (parity + 1) * N)
                value = jnp.concatenate([slab(mode)[rows, :] for mode in modes], axis=1)
                parts.append(table_first(vx[parity], value * ratio[parity]))
            for side in range(2):
                result = parts[0] + parts[1] if side == 0 else parts[0] - parts[1]
                for k in range(2):
                    slab(modes[k])[side * N : (side + 1) * N, :] = result[:, k * H : (k + 1) * H]
        send_half(me, half, home, target, back_sem, ret_sem)
    send_home(me, home, target, back_sem, ret_sem, own_sem)
    wait_bytes(ret.at[pl.ds(0, 511)], ret_sem)
    wait_bytes(ret.at[pl.ds(0, 511)], back_sem)
    wait_bytes(ret.at[pl.ds(0, 511)], send_sem)


def update(
    obj, prb, ret, vy, vz, out, part, pair, total, early, near,
    pair_send, pair_recv, early_send, early_recv, near_send, near_recv,
):
    me = place()
    core, other, y_hi = me["core"], 1 - me["core"], me["y_hi"]
    barrier = pltpu.get_barrier_semaphore()
    greet(barrier, me, mode_peer)
    ways = (1, 3)

    def chip(d):
        return {"mode": (y_hi + d) % 4 * 2 + core}

    def to_core(x):
        return ship(
            part.at[other, x], pair.at[x], pair_send.at[x], pair_recv.at[x], {"mode": y_hi * 2 + other}
        )

    def early_to(x, way):
        return ship(
            total.at[x, (y_hi + 2) % 4, way], early.at[x, way], early_send.at[x, way], early_recv.at[x, way],
            chip(ways[way]),
        )

    def near_to(x, way):
        return ship(
            total.at[x, (y_hi + ways[way]) % 4], near.at[x, way], near_send.at[x, way], near_recv.at[x, way],
            chip(ways[way]),
        )

    def first(x):
        to_core(x).wait_recv()
        total[x] = part[core, x] + pair[x]
        for way in range(2):
            early_to(x, way).start()

    def second(x):
        for way in range(2):
            early_to(x, way).wait_recv()
            total[x, (y_hi + ways[way]) % 4, way] += early[x, way]
            near_to(x, way).start()

    for two in range(2):
        columns = []
        for half in range(2):
            flat = ret.at[pl.ds(half * N, N)].reshape(N * 8, H)
            pieces = []
            for parity in range(2):
                blocks = [
                    [flat[pl.ds(parity * 8 + c * 4 + 2 * two + k, H, stride=16), :] for k in range(2)]
                    for c in range(2)
                ]
                value = jnp.concatenate([jnp.concatenate(b, axis=1) for b in blocks], axis=0)
                pieces.append(table_first(vy[parity], value))
            columns.append((pieces[0] + pieces[1], pieces[0] - pieces[1]))
        for k in range(2):
            x = 2 * two + k
            lanes = slice(k * H, (k + 1) * H)
            lines = []
            for half in range(2):
                top, bottom = columns[half]
                re = jnp.concatenate([top[:H, lanes], bottom[:H, lanes]], axis=0)
                im = jnp.concatenate([top[H:, lanes], bottom[H:, lanes]], axis=0)
                lines.append(table_last(jnp.concatenate([re, im], axis=1), vz[half]))
            low, high = lines[0] + lines[1], lines[0] - lines[1]
            p_re, p_im, e_re, e_im = exit_wave(obj, prb, x)
            d_re = jnp.concatenate([low[:, :H], high[:, :H]], axis=1) - e_re
            d_im = jnp.concatenate([low[:, H:], high[:, H:]], axis=1) - e_im
            g_re = p_re * d_re + p_im * d_im
            g_im = p_re * d_im - p_im * d_re
            for chunk in range(8):
                rows = slice(32 * chunk, 32 * chunk + 32)
                part[chunk % 2, x, chunk // 2, 0] = g_re[rows]
                part[chunk % 2, x, chunk // 2, 1] = g_im[rows]
            if x == 0:
                pl.semaphore_wait(barrier, 7)
            to_core(x).start()
            if x > 0:
                first(x - 1)
            if x > 1:
                second(x - 2)
    first(3)
    second(2)
    second(3)
    for x in range(4):
        for way in range(2):
            near_to(x, way).wait_recv()
        out[:, x] = total[x, y_hi] + (near[x, 0] + near[x, 1])
    for x in range(4):
        to_core(x).wait_send()
        for way in range(2):
            early_to(x, way).wait_send()
            near_to(x, way).wait_send()


def call(body, name, number, inputs, results, scratch):
    fields = dict(collective_id=number, has_side_effects=True) if number is not None else {}
    vmem = pl.BlockSpec(memory_space=pltpu.VMEM)
    return pl.pallas_call(
        body,
        out_shape=[jax.ShapeDtypeStruct(shape, F32) for shape in results],
        in_specs=[vmem] * len(inputs),
        out_specs=[vmem] * len(results),
        scratch_shapes=scratch,
        compiler_params=pltpu.CompilerParams(vmem_limit_bytes=40 * 2**20, **fields),
        name=name,
    )(*inputs)


def shards(object_field, probes, measured):
    weights, rows = tables()
    wz, wy, wx, vx, vy, vz = [jnp.asarray(weights[k]) for k in range(6)]
    vmem, dma, regular = pltpu.VMEM, pltpu.SemaphoreType.DMA, pltpu.SemaphoreType.REGULAR
    prb = probes[0]
    tiles = (512, 8, H)
    send, root = call(
        transform_zy, "transform_zy", None, (object_field, prb, measured, wz, wy, jnp.asarray(rows)),
        (tiles, (N, H)), [],
    )
    (ret,) = call(
        exchange, "exchange", 0, (send, root, wx, vx), (tiles,),
        [vmem(tiles, F32), regular, regular, dma, dma, dma, dma, dma],
    )
    (gradient,) = call(
        update, "update", 1, (object_field, prb, ret, vy, vz), ((2, 4, 32, N),),
        [
            vmem((2, 4, 4, 2, 32, N), F32),
            vmem((4, 4, 2, 32, N), F32),
            vmem((4, 4, 2, 32, N), F32),
            vmem((4, 2, 32, N), F32),
            vmem((4, 2, 2, 32, N), F32),
            dma((4,)), dma((4,)), dma((4, 2)), dma((4, 2)), dma((4, 2)), dma((4, 2)),
        ],
    )
    return gradient


def solution(mesh):
    return jax.shard_map(
        shards,
        mesh=mesh,
        in_specs=(
            P(None, "pen", None, None),
            P("mode", None, "pen", None, None),
            P(None, "pen", None),
        ),
        out_specs=P(None, "pen", "mode", None),
        check_vma=False,
    )
```

```python
import functools
import math

import jax
import jax.numpy as jnp
import ml_dtypes
import numpy as np
from jax import lax
from jax.experimental import pallas as pl
from jax.experimental.pallas import tpu as pltpu
from jax.sharding import PartitionSpec as P

DAMP = 0.1
N = 256
H = N // 2
F32 = jnp.float32
BF16 = jnp.bfloat16
MESH = pl.DeviceIdType.MESH


def forward_matrix(parity):
    freq = 2 * np.arange(H) + parity
    angle = 2.0 * math.pi / N * ((freq[:, None] * np.arange(H)[None, :]) % N)
    cosine, sine = np.cos(angle) / math.sqrt(N), np.sin(angle) / math.sqrt(N)
    return np.block([[cosine, sine], [-sine, cosine]])


def inverse_matrix(parity):
    return forward_matrix(parity).T


def split(matrix):
    high = matrix.astype(ml_dtypes.bfloat16)
    low = (matrix - high.astype(np.float64)).astype(ml_dtypes.bfloat16)
    return np.stack([high, low])


def tables():
    slab, part, row = np.meshgrid(np.arange(H // 4), np.arange(2), np.arange(4), indexing="ij")
    order = (part * H + slab * 4 + row).reshape(-1)
    sets = []
    for parity in range(2):
        fwd, inv = forward_matrix(parity), inverse_matrix(parity)
        sets.append(
            [split(fwd.T), split(fwd), split(fwd[:, order]), split(inv[order, :]), split(inv), split(inv.T)]
        )
    return np.stack([np.stack([sets[0][k], sets[1][k]]) for k in range(6)])


def halves(value):
    high = value.astype(BF16)
    return high, (value - high.astype(F32)).astype(BF16)


def dot(left, right):
    return jnp.dot(left, right, preferred_element_type=F32)


def table_first(table, value):
    high, low = halves(value)
    return dot(table[0], high) + (dot(table[0], low) + dot(table[1], high))


def table_last(value, table):
    high, low = halves(value)
    return dot(high, table[0]) + (dot(low, table[0]) + dot(high, table[1]))


def place():
    mode, pen = lax.axis_index("mode"), lax.axis_index("pen")
    return dict(
        mode=mode, pen=pen, y_hi=mode // 2, core=mode % 2, y=(mode // 2) * 2 + pen // 32, z=(pen // 4) % 8, x=pen % 4
    )


def chip_at(me, step):
    t = (step * 181) % 256
    x, y, z = (me["x"] + t % 4) % 4, (me["y"] + (t // 4) % 8) % 8, (me["z"] + t // 32) % 8
    return y // 2, (y % 2) * 32 + z * 4 + x


def z_peer(me, step):
    return {"pen": me["pen"] // 32 * 32 + (me["z"] + step) % 8 * 4 + me["x"]}


def xy_peer(me, step):
    other = (me["pen"] // 32 * 4 + me["x"] + step) % 8
    return {"pen": other // 4 * 32 + me["z"] * 4 + other % 4}


def mode_peer(me, step):
    return {"mode": (me["mode"] + step) % 8}


def greet(semaphore, me, *kinds):
    for kind in kinds:
        for step in range(1, 8):
            pl.semaphore_signal(semaphore, inc=1, device_id=kind(me, step), device_id_type=MESH)


def meet_all(me, lines, planes):
    barrier = pltpu.get_barrier_semaphore()
    greet(barrier, me, mode_peer, z_peer, xy_peer)
    pl.semaphore_wait(barrier, 21)
    greet(lines, me, z_peer)
    pl.semaphore_wait(lines, 7)
    greet(planes, me, xy_peer)
    pl.semaphore_wait(planes, 7)


def ship(source, target, ssem, rsem, device):
    return pltpu.make_async_remote_copy(
        src_ref=source, dst_ref=target, send_sem=ssem, recv_sem=rsem, device_id=device, device_id_type=MESH
    )


def wait_bytes(ref, sem):
    pltpu.make_async_copy(ref, ref, sem).wait()


def exit_wave(obj, prb, x):
    p_re, p_im = prb[0, x].astype(F32), prb[1, x].astype(F32)
    o_re, o_im = obj[0, x].astype(F32), obj[1, x].astype(F32)
    return p_re, p_im, p_re * o_re - p_im * o_im, p_re * o_im + p_im * o_re


def magnitudes(me, own):
    own = jnp.sqrt(own)
    row, column = (lax.broadcasted_iota(jnp.int32, (N, N), k) for k in range(2))
    evens_first = (column == row % H * 2 + row // H).astype(F32)
    rows = jnp.dot(evens_first, own, precision=lax.Precision.HIGHEST, preferred_element_type=F32)
    row, column = (lax.broadcasted_iota(jnp.int32, (N, H), k) for k in range(2))
    chosen = (row == column * 2 + me["core"]).astype(F32)
    return jnp.dot(rows, chosen, precision=lax.Precision.HIGHEST, preferred_element_type=F32)


def transform_zy(
    obj_in, prb_in, meas_in, wz_in, wy_in, send, own, obj, prb, meas, wz, wy, obj_sem, prb_sem, sem
):
    me = place()

    def obj_row(x):
        return pltpu.make_async_copy(obj_in.at[:, x], obj.at[:, x], obj_sem.at[x])

    def prb_row(x):
        return pltpu.make_async_copy(prb_in.at[:, x], prb.at[:, x], prb_sem.at[x])

    table_z = pltpu.make_async_copy(wz_in, wz, sem.at[0])
    table_y = pltpu.make_async_copy(wy_in, wy, sem.at[1])
    intensities = [
        pltpu.make_async_copy(meas_in.at[pl.ds(64 * k, 64)], meas.at[pl.ds(64 * k, 64)], sem.at[2 + k]) for k in range(4)
    ]
    for x in range(2):
        obj_row(x).start()
        prb_row(x).start()
    table_z.start()
    table_y.start()
    for x in range(2, 4):
        obj_row(x).start()
        prb_row(x).start()
    for k in range(4):
        intensities[k].start()

    for half in range(2):
        for two in range(2):
            lines = []
            for x in (2 * two, 2 * two + 1):
                if half == 0:
                    obj_row(x).wait()
                    prb_row(x).wait()
                _, _, e_re, e_im = exit_wave(obj, prb, x)
                if half == 0:
                    mixed = jnp.concatenate([e_re[:, :H] + e_re[:, H:], e_im[:, :H] + e_im[:, H:]], axis=1)
                else:
                    mixed = jnp.concatenate([e_re[:, :H] - e_re[:, H:], e_im[:, :H] - e_im[:, H:]], axis=1)
                if half == 0 and x == 0:
                    table_z.wait()
                    table_y.wait()
                lines.append(table_last(mixed, wz[half]))
            re = jnp.concatenate([lines[0][:, :H], lines[1][:, :H]], axis=1)
            im = jnp.concatenate([lines[0][:, H:], lines[1][:, H:]], axis=1)
            for parity in range(2):
                if parity == 0:
                    mixed = jnp.concatenate([re[:H] + re[H:], im[:H] + im[H:]], axis=0)
                else:
                    mixed = jnp.concatenate([re[:H] - re[H:], im[:H] - im[H:]], axis=0)
                result = table_first(wy[parity], mixed)
                flat = send.at[pl.ds(half * N, N)].reshape(N * 8, H)
                for c in range(2):
                    for k in range(2):
                        rows = pl.ds(parity * 8 + c * 4 + 2 * two + k, H, stride=16)
                        flat[rows, :] = result[c * H : (c + 1) * H, k * H : (k + 1) * H]
    for k in range(4):
        intensities[k].wait()
    own[...] = meas[:, pl.ds(me["y_hi"], 1), :].reshape(N, N)


def send_half(me, half, source, target, send_sem, recv_sem):
    @pl.loop(1, 256)
    def _(step):
        y_hi, pen = chip_at(me, step)
        mode = y_hi * 2 + half
        ship(source(mode, pen), target, send_sem, recv_sem, {"mode": mode, "pen": pen}).start()


def send_home(me, source, target, send_sem, recv_sem, own_sem):
    sibling = me["y_hi"] * 2 + 1 - me["core"]
    ship(source(sibling, me["pen"]), target, send_sem, recv_sem, {"mode": sibling}).start()
    own = pltpu.make_async_copy(source(me["mode"], me["pen"]), target, own_sem)
    own.start()
    own.wait()


def exchange(
    send, own, wx, vx, ret, recv, lines, planes, send_sem, recv_sem, back_sem, ret_sem, own_sem
):
    me = place()
    meet_all(me, lines, planes)

    def tile(mode, pen):
        return send.at[mode % 2 * N + 4 * pen + mode // 2]

    landing = recv.at[me["mode"] * 64 + me["pen"]]
    for half in range(2):
        send_half(me, half, tile, landing, send_sem, recv_sem)
    send_home(me, tile, landing, send_sem, recv_sem, own_sem)
    root = magnitudes(me, own[...])
    wait_bytes(recv.at[pl.ds(0, 511)], recv_sem)

    def slab(mode):
        return recv.at[pl.ds(64 * mode, 64)].reshape(2 * N, H)

    power = [jnp.zeros((H, H), F32), jnp.zeros((H, H), F32)]
    for two in range(4):
        value = jnp.concatenate([slab(2 * two + k)[...] for k in range(2)], axis=1)
        top, bottom = value[:N], value[N:]
        for parity in range(2):
            result = table_first(wx[parity], top + bottom if parity == 0 else top - bottom)
            for k in range(2):
                slab(2 * two + k)[parity * N : (parity + 1) * N, :] = result[:, k * H : (k + 1) * H]
            square = result * result
            square = square[:H] + square[H:]
            power[parity] = power[parity] + (square[:, :H] + square[:, H:])
    ratio = [root[parity * H : (parity + 1) * H] / jnp.sqrt(power[parity] + DAMP) for parity in range(2)]
    ratio = [jnp.concatenate([r, r], axis=0) for r in ratio]
    ratio = [jnp.concatenate([r, r], axis=1) for r in ratio]

    def home(mode, pen):
        return recv.at[mode * 64 + pen]

    target = ret.at[me["core"] * N + 4 * me["pen"] + me["y_hi"]]
    for half in range(2):
        for two in range(2):
            modes = (4 * two + half, 4 * two + 2 + half)
            parts = []
            for parity in range(2):
                rows = slice(parity * N, (parity + 1) * N)
                value = jnp.concatenate([slab(mode)[rows, :] for mode in modes], axis=1)
                parts.append(table_first(vx[parity], value * ratio[parity]))
            for side in range(2):
                result = parts[0] + parts[1] if side == 0 else parts[0] - parts[1]
                for k in range(2):
                    slab(modes[k])[side * N : (side + 1) * N, :] = result[:, k * H : (k + 1) * H]
        send_half(me, half, home, target, back_sem, ret_sem)
    send_home(me, home, target, back_sem, ret_sem, own_sem)
    wait_bytes(ret.at[pl.ds(0, 511)], ret_sem)
    wait_bytes(ret.at[pl.ds(0, 511)], back_sem)
    wait_bytes(ret.at[pl.ds(0, 511)], send_sem)


def update(
    obj, prb, ret, vy, vz, out, part, pair, total, early, near,
    pair_send, pair_recv, early_send, early_recv, near_send, near_recv,
):
    me = place()
    core, other, y_hi = me["core"], 1 - me["core"], me["y_hi"]
    barrier = pltpu.get_barrier_semaphore()
    greet(barrier, me, mode_peer)
    ways = (1, 3)

    def chip(d):
        return {"mode": (y_hi + d) % 4 * 2 + core}

    def to_core(x):
        return ship(
            part.at[other, x], pair.at[x], pair_send.at[x], pair_recv.at[x], {"mode": y_hi * 2 + other}
        )

    def early_to(x, way):
        return ship(
            total.at[x, (y_hi + 2) % 4, way], early.at[x, way], early_send.at[x, way], early_recv.at[x, way],
            chip(ways[way]),
        )

    def near_to(x, way):
        return ship(
            total.at[x, (y_hi + ways[way]) % 4], near.at[x, way], near_send.at[x, way], near_recv.at[x, way],
            chip(ways[way]),
        )

    def first(x):
        to_core(x).wait_recv()
        total[x] = part[core, x] + pair[x]
        for way in range(2):
            early_to(x, way).start()

    def second(x):
        for way in range(2):
            early_to(x, way).wait_recv()
            total[x, (y_hi + ways[way]) % 4, way] += early[x, way]
            near_to(x, way).start()

    for two in range(2):
        columns = []
        for half in range(2):
            flat = ret.at[pl.ds(half * N, N)].reshape(N * 8, H)
            pieces = []
            for parity in range(2):
                blocks = [
                    [flat[pl.ds(parity * 8 + c * 4 + 2 * two + k, H, stride=16), :] for k in range(2)]
                    for c in range(2)
                ]
                value = jnp.concatenate([jnp.concatenate(b, axis=1) for b in blocks], axis=0)
                pieces.append(table_first(vy[parity], value))
            columns.append((pieces[0] + pieces[1], pieces[0] - pieces[1]))
        for k in range(2):
            x = 2 * two + k
            lanes = slice(k * H, (k + 1) * H)
            lines = []
            for half in range(2):
                top, bottom = columns[half]
                re = jnp.concatenate([top[:H, lanes], bottom[:H, lanes]], axis=0)
                im = jnp.concatenate([top[H:, lanes], bottom[H:, lanes]], axis=0)
                lines.append(table_last(jnp.concatenate([re, im], axis=1), vz[half]))
            low, high = lines[0] + lines[1], lines[0] - lines[1]
            p_re, p_im, e_re, e_im = exit_wave(obj, prb, x)
            d_re = jnp.concatenate([low[:, :H], high[:, :H]], axis=1) - e_re
            d_im = jnp.concatenate([low[:, H:], high[:, H:]], axis=1) - e_im
            g_re = p_re * d_re + p_im * d_im
            g_im = p_re * d_im - p_im * d_re
            for chunk in range(8):
                rows = slice(32 * chunk, 32 * chunk + 32)
                part[chunk % 2, x, chunk // 2, 0] = g_re[rows]
                part[chunk % 2, x, chunk // 2, 1] = g_im[rows]
            if x == 0:
                pl.semaphore_wait(barrier, 7)
            to_core(x).start()
            if x > 0:
                first(x - 1)
            if x > 1:
                second(x - 2)
    first(3)
    second(2)
    second(3)
    for x in range(4):
        for way in range(2):
            near_to(x, way).wait_recv()
        out[:, x] = total[x, y_hi] + (near[x, 0] + near[x, 1])
    for x in range(4):
        to_core(x).wait_send()
        for way in range(2):
            early_to(x, way).wait_send()
            near_to(x, way).wait_send()


def call(body, name, number, inputs, results, scratch, limit=40, space=pltpu.VMEM):
    fields = dict(collective_id=number, has_side_effects=True) if number is not None else {}
    return pl.pallas_call(
        body,
        out_shape=[jax.ShapeDtypeStruct(shape, F32) for shape in results],
        in_specs=[pl.BlockSpec(memory_space=space)] * len(inputs),
        out_specs=[pl.BlockSpec(memory_space=pltpu.VMEM)] * len(results),
        scratch_shapes=scratch,
        compiler_params=pltpu.CompilerParams(vmem_limit_bytes=limit * 2**20, **fields),
        name=name,
    )(*inputs)


def shards(object_field, probes, measured):
    weights = tables()
    wz, wy, wx, vx, vy, vz = [jnp.asarray(weights[k]) for k in range(6)]
    vmem, dma, regular = pltpu.VMEM, pltpu.SemaphoreType.DMA, pltpu.SemaphoreType.REGULAR
    prb = probes[0]
    tiles = (512, 8, H)
    slab = (2, 4, N, N)
    send, own = call(
        transform_zy, "transform_zy", None, tuple(
            pltpu.with_memory_space_constraint(a, pltpu.HBM) for a in (object_field, prb, measured, wz, wy)
        ), (tiles, (N, N)),
        [
            vmem(slab, BF16), vmem(slab, BF16), vmem((N, 4, N), F32), vmem(wz.shape, BF16), vmem(wy.shape, BF16),
            dma((4,)), dma((4,)), dma((6,)),
        ],
        space=pl.ANY,
    )
    (ret,) = call(
        exchange, "exchange", 0, (send, own, wx, vx), (tiles,),
        [vmem(tiles, F32), regular, regular, dma, dma, dma, dma, dma],
    )
    (gradient,) = call(
        update, "update", 1, (object_field, prb, ret, vy, vz), ((2, 4, 32, N),),
        [
            vmem((2, 4, 4, 2, 32, N), F32),
            vmem((4, 4, 2, 32, N), F32),
            vmem((4, 4, 2, 32, N), F32),
            vmem((4, 2, 32, N), F32),
            vmem((4, 2, 2, 32, N), F32),
            dma((4,)), dma((4,)), dma((4, 2)), dma((4, 2)), dma((4, 2)), dma((4, 2)),
        ],
    )
    return gradient


def solution(mesh):
    return jax.shard_map(
        shards,
        mesh=mesh,
        in_specs=(
            P(None, "pen", None, None),
            P("mode", None, "pen", None, None),
            P(None, "pen", None),
        ),
        out_specs=P(None, "pen", "mode", None),
        check_vma=False,
    )
```

```python
import functools
import math

import jax
import jax.numpy as jnp
import ml_dtypes
import numpy as np
from jax import lax
from jax.experimental import pallas as pl
from jax.experimental.pallas import tpu as pltpu
from jax.sharding import PartitionSpec as P

DAMP = 0.1
N = 256
H = N // 2
F32 = jnp.float32
BF16 = jnp.bfloat16
MESH = pl.DeviceIdType.MESH


def forward_matrix(parity):
    freq = 2 * np.arange(H) + parity
    angle = 2.0 * math.pi / N * ((freq[:, None] * np.arange(H)[None, :]) % N)
    cosine, sine = np.cos(angle) / math.sqrt(N), np.sin(angle) / math.sqrt(N)
    return np.block([[cosine, sine], [-sine, cosine]])


def inverse_matrix(parity):
    return forward_matrix(parity).T


def split(matrix):
    high = matrix.astype(ml_dtypes.bfloat16)
    low = (matrix - high.astype(np.float64)).astype(ml_dtypes.bfloat16)
    return np.stack([high, low])


def tables():
    slab, part, row = np.meshgrid(np.arange(H // 4), np.arange(2), np.arange(4), indexing="ij")
    order = (part * H + slab * 4 + row).reshape(-1)
    sets = []
    for parity in range(2):
        fwd, inv = forward_matrix(parity), inverse_matrix(parity)
        sets.append(
            [split(fwd.T), split(fwd), split(fwd[:, order]), split(inv[order, :]), split(inv), split(inv.T)]
        )
    return np.stack([np.stack([sets[0][k], sets[1][k]]) for k in range(6)])


def halves(value):
    high = value.astype(BF16)
    return high, (value - high.astype(F32)).astype(BF16)


def dot(left, right):
    return jnp.dot(left, right, preferred_element_type=F32)


def table_first(table, value):
    high, low = halves(value)
    return dot(table[0], high) + (dot(table[0], low) + dot(table[1], high))


def table_last(value, table):
    high, low = halves(value)
    return dot(high, table[0]) + (dot(low, table[0]) + dot(high, table[1]))


def place():
    mode, pen = lax.axis_index("mode"), lax.axis_index("pen")
    return dict(
        mode=mode, pen=pen, y_hi=mode // 2, core=mode % 2, y=(mode // 2) * 2 + pen // 32, z=(pen // 4) % 8, x=pen % 4
    )


def chip_at(me, step):
    t = (step * 181) % 256
    x, y, z = (me["x"] + t % 4) % 4, (me["y"] + (t // 4) % 8) % 8, (me["z"] + t // 32) % 8
    return y // 2, (y % 2) * 32 + z * 4 + x


def z_peer(me, step):
    return {"pen": me["pen"] // 32 * 32 + (me["z"] + step) % 8 * 4 + me["x"]}


def xy_peer(me, step):
    other = (me["pen"] // 32 * 4 + me["x"] + step) % 8
    return {"pen": other // 4 * 32 + me["z"] * 4 + other % 4}


def mode_peer(me, step):
    return {"mode": (me["mode"] + step) % 8}


def greet(semaphore, me, *kinds):
    for kind in kinds:
        for step in range(1, 8):
            pl.semaphore_signal(semaphore, inc=1, device_id=kind(me, step), device_id_type=MESH)


def ship(source, target, ssem, rsem, device):
    return pltpu.make_async_remote_copy(
        src_ref=source, dst_ref=target, send_sem=ssem, recv_sem=rsem, device_id=device, device_id_type=MESH
    )


def wait_bytes(ref, sem):
    pltpu.make_async_copy(ref, ref, sem).wait()


def exit_wave(obj, prb, x):
    p_re, p_im = prb[0, x].astype(F32), prb[1, x].astype(F32)
    o_re, o_im = obj[0, x].astype(F32), obj[1, x].astype(F32)
    return p_re, p_im, p_re * o_re - p_im * o_im, p_re * o_im + p_im * o_re


def magnitudes(me, own):
    own = jnp.sqrt(own)
    row, column = (lax.broadcasted_iota(jnp.int32, (N, N), k) for k in range(2))
    evens_first = (column == row % H * 2 + row // H).astype(F32)
    rows = jnp.dot(evens_first, own, precision=lax.Precision.HIGHEST, preferred_element_type=F32)
    row, column = (lax.broadcasted_iota(jnp.int32, (N, H), k) for k in range(2))
    chosen = (row == column * 2 + me["core"]).astype(F32)
    return jnp.dot(rows, chosen, precision=lax.Precision.HIGHEST, preferred_element_type=F32)


def transform_zy(
    obj_in, prb_in, meas_in, wz_in, wy_in, send, own, obj, prb, meas, wz, wy, obj_sem, prb_sem, sem
):
    me = place()

    def obj_row(x):
        return pltpu.make_async_copy(obj_in.at[:, x], obj.at[:, x], obj_sem.at[x])

    def prb_row(x):
        return pltpu.make_async_copy(prb_in.at[:, x], prb.at[:, x], prb_sem.at[x])

    table_z = pltpu.make_async_copy(wz_in, wz, sem.at[0])
    table_y = pltpu.make_async_copy(wy_in, wy, sem.at[1])
    intensities = [
        pltpu.make_async_copy(meas_in.at[pl.ds(64 * k, 64)], meas.at[pl.ds(64 * k, 64)], sem.at[2 + k]) for k in range(4)
    ]
    for x in range(2):
        obj_row(x).start()
        prb_row(x).start()
    table_z.start()
    table_y.start()
    for x in range(2, 4):
        obj_row(x).start()
        prb_row(x).start()
    for k in range(4):
        intensities[k].start()

    for half in range(2):
        for two in range(2):
            lines = []
            for x in (2 * two, 2 * two + 1):
                if half == 0:
                    obj_row(x).wait()
                    prb_row(x).wait()
                _, _, e_re, e_im = exit_wave(obj, prb, x)
                if half == 0:
                    mixed = jnp.concatenate([e_re[:, :H] + e_re[:, H:], e_im[:, :H] + e_im[:, H:]], axis=1)
                else:
                    mixed = jnp.concatenate([e_re[:, :H] - e_re[:, H:], e_im[:, :H] - e_im[:, H:]], axis=1)
                if half == 0 and x == 0:
                    table_z.wait()
                    table_y.wait()
                lines.append(table_last(mixed, wz[half]))
            re = jnp.concatenate([lines[0][:, :H], lines[1][:, :H]], axis=1)
            im = jnp.concatenate([lines[0][:, H:], lines[1][:, H:]], axis=1)
            for parity in range(2):
                if parity == 0:
                    mixed = jnp.concatenate([re[:H] + re[H:], im[:H] + im[H:]], axis=0)
                else:
                    mixed = jnp.concatenate([re[:H] - re[H:], im[:H] - im[H:]], axis=0)
                result = table_first(wy[parity], mixed)
                flat = send.at[pl.ds(half * N, N)].reshape(N * 8, H)
                for c in range(2):
                    for k in range(2):
                        rows = pl.ds(parity * 8 + c * 4 + 2 * two + k, H, stride=16)
                        flat[rows, :] = result[c * H : (c + 1) * H, k * H : (k + 1) * H]
    for k in range(4):
        intensities[k].wait()
    own[...] = meas[:, pl.ds(me["y_hi"], 1), :].reshape(N, N)


def send_half(me, half, source, target, send_sem, recv_sem):
    @pl.loop(1, 256)
    def _(step):
        y_hi, pen = chip_at(me, step)
        mode = y_hi * 2 + half
        ship(source(mode, pen), target, send_sem, recv_sem, {"mode": mode, "pen": pen}).start()


def send_home(me, source, target, send_sem, recv_sem, own_sem):
    sibling = me["y_hi"] * 2 + 1 - me["core"]
    ship(source(sibling, me["pen"]), target, send_sem, recv_sem, {"mode": sibling}).start()
    own = pltpu.make_async_copy(source(me["mode"], me["pen"]), target, own_sem)
    own.start()
    own.wait()


def exchange(
    send, own, wx, vx, ret, recv, lines, planes, send_sem, recv_sem, back_sem, ret_sem, own_sem
):
    me = place()
    barrier = pltpu.get_barrier_semaphore()

    def tile(mode, pen):
        return send.at[mode % 2 * N + 4 * pen + mode // 2]

    landing = recv.at[me["mode"] * 64 + me["pen"]]

    def pass_on(half, by_chip, by_xy):
        mode = (me["y_hi"] + by_chip % 4) % 4 * 2 + half
        z, xy = (me["z"] + by_chip // 4) % 8, (me["pen"] // 32 * 4 + me["x"] + by_xy) % 8
        pen = xy // 4 * 32 + z * 4 + xy % 4

        @pl.when((mode != me["mode"]) | (pen != me["pen"]))
        def _():
            ship(tile(mode, pen), landing, send_sem, recv_sem, {"mode": mode, "pen": pen}).start()

    greet(barrier, me, mode_peer, z_peer, xy_peer)
    pl.semaphore_wait(barrier, 21)
    greet(lines, me, z_peer)
    pl.semaphore_wait(lines, 7)
    greet(planes, me, xy_peer)

    @pl.loop(0, 32)
    def _(step):
        pass_on(0, step * 13 % 32, 0)

    pl.semaphore_wait(planes, 7)

    @pl.loop(0, 224)
    def _(step):
        t = step * 93 % 224
        pass_on(0, t % 32, 1 + t // 32)

    @pl.loop(0, 256)
    def _(step):
        t = step * 181 % 256
        pass_on(1, t % 32, t // 32)

    own_tile = pltpu.make_async_copy(tile(me["mode"], me["pen"]), landing, own_sem)
    own_tile.start()
    own_tile.wait()
    root = magnitudes(me, own[...])
    wait_bytes(recv.at[pl.ds(0, 511)], recv_sem)

    def slab(mode):
        return recv.at[pl.ds(64 * mode, 64)].reshape(2 * N, H)

    power = [jnp.zeros((H, H), F32), jnp.zeros((H, H), F32)]
    for two in range(4):
        value = jnp.concatenate([slab(2 * two + k)[...] for k in range(2)], axis=1)
        top, bottom = value[:N], value[N:]
        for parity in range(2):
            result = table_first(wx[parity], top + bottom if parity == 0 else top - bottom)
            for k in range(2):
                slab(2 * two + k)[parity * N : (parity + 1) * N, :] = result[:, k * H : (k + 1) * H]
            square = result * result
            square = square[:H] + square[H:]
            power[parity] = power[parity] + (square[:, :H] + square[:, H:])
    ratio = [root[parity * H : (parity + 1) * H] / jnp.sqrt(power[parity] + DAMP) for parity in range(2)]
    ratio = [jnp.concatenate([r, r], axis=0) for r in ratio]
    ratio = [jnp.concatenate([r, r], axis=1) for r in ratio]

    def home(mode, pen):
        return recv.at[mode * 64 + pen]

    target = ret.at[me["core"] * N + 4 * me["pen"] + me["y_hi"]]
    for half in range(2):
        for two in range(2):
            modes = (4 * two + half, 4 * two + 2 + half)
            parts = []
            for parity in range(2):
                rows = slice(parity * N, (parity + 1) * N)
                value = jnp.concatenate([slab(mode)[rows, :] for mode in modes], axis=1)
                parts.append(table_first(vx[parity], value * ratio[parity]))
            for side in range(2):
                result = parts[0] + parts[1] if side == 0 else parts[0] - parts[1]
                for k in range(2):
                    slab(modes[k])[side * N : (side + 1) * N, :] = result[:, k * H : (k + 1) * H]
        send_half(me, half, home, target, back_sem, ret_sem)
    send_home(me, home, target, back_sem, ret_sem, own_sem)
    wait_bytes(ret.at[pl.ds(0, 511)], ret_sem)
    wait_bytes(ret.at[pl.ds(0, 511)], back_sem)
    wait_bytes(ret.at[pl.ds(0, 511)], send_sem)


def update(
    obj, prb, ret, vy, vz, out, part, pair, total, early, near,
    pair_send, pair_recv, early_send, early_recv, near_send, near_recv,
):
    me = place()
    core, other, y_hi = me["core"], 1 - me["core"], me["y_hi"]
    barrier = pltpu.get_barrier_semaphore()
    ways = (1, 3)

    def chip(d):
        return {"mode": (y_hi + d) % 4 * 2 + core}

    for device in ({"mode": y_hi * 2 + other}, chip(1), chip(3)):
        pl.semaphore_signal(barrier, inc=1, device_id=device, device_id_type=MESH)

    def to_core(x):
        return ship(
            part.at[other, x], pair.at[x], pair_send.at[x], pair_recv.at[x], {"mode": y_hi * 2 + other}
        )

    def early_to(x, way):
        return ship(
            total.at[x, (y_hi + 2) % 4, way], early.at[x, way], early_send.at[x, way], early_recv.at[x, way],
            chip(ways[way]),
        )

    def near_to(x, way):
        return ship(
            total.at[x, (y_hi + ways[way]) % 4], near.at[x, way], near_send.at[x, way], near_recv.at[x, way],
            chip(ways[way]),
        )

    def first(x):
        to_core(x).wait_recv()
        total[x] = part[core, x] + pair[x]
        for way in range(2):
            early_to(x, way).start()

    def second(x):
        for way in range(2):
            early_to(x, way).wait_recv()
            total[x, (y_hi + ways[way]) % 4, way] += early[x, way]
            near_to(x, way).start()

    for two in range(2):
        columns = []
        for half in range(2):
            flat = ret.at[pl.ds(half * N, N)].reshape(N * 8, H)
            pieces = []
            for parity in range(2):
                blocks = [
                    [flat[pl.ds(parity * 8 + c * 4 + 2 * two + k, H, stride=16), :] for k in range(2)]
                    for c in range(2)
                ]
                value = jnp.concatenate([jnp.concatenate(b, axis=1) for b in blocks], axis=0)
                pieces.append(table_first(vy[parity], value))
            columns.append((pieces[0] + pieces[1], pieces[0] - pieces[1]))
        for k in range(2):
            x = 2 * two + k
            lanes = slice(k * H, (k + 1) * H)
            lines = []
            for half in range(2):
                top, bottom = columns[half]
                re = jnp.concatenate([top[:H, lanes], bottom[:H, lanes]], axis=0)
                im = jnp.concatenate([top[H:, lanes], bottom[H:, lanes]], axis=0)
                lines.append(table_last(jnp.concatenate([re, im], axis=1), vz[half]))
            low, high = lines[0] + lines[1], lines[0] - lines[1]
            p_re, p_im, e_re, e_im = exit_wave(obj, prb, x)
            d_re = jnp.concatenate([low[:, :H], high[:, :H]], axis=1) - e_re
            d_im = jnp.concatenate([low[:, H:], high[:, H:]], axis=1) - e_im
            g_re = p_re * d_re + p_im * d_im
            g_im = p_re * d_im - p_im * d_re
            for chunk in range(8):
                rows = slice(32 * chunk, 32 * chunk + 32)
                part[chunk % 2, x, chunk // 2, 0] = g_re[rows]
                part[chunk % 2, x, chunk // 2, 1] = g_im[rows]
            if x == 0:
                pl.semaphore_wait(barrier, 3)
            to_core(x).start()
            if x > 0:
                first(x - 1)
            if x > 1:
                second(x - 2)
    first(3)
    second(2)
    second(3)
    for x in range(4):
        for way in range(2):
            near_to(x, way).wait_recv()
        out[:, x] = total[x, y_hi] + (near[x, 0] + near[x, 1])
    for x in range(4):
        to_core(x).wait_send()
        for way in range(2):
            early_to(x, way).wait_send()
            near_to(x, way).wait_send()


def call(body, name, number, inputs, results, scratch, limit=40, space=pltpu.VMEM):
    fields = dict(collective_id=number, has_side_effects=True) if number is not None else {}
    return pl.pallas_call(
        body,
        out_shape=[jax.ShapeDtypeStruct(shape, F32) for shape in results],
        in_specs=[pl.BlockSpec(memory_space=space)] * len(inputs),
        out_specs=[pl.BlockSpec(memory_space=pltpu.VMEM)] * len(results),
        scratch_shapes=scratch,
        compiler_params=pltpu.CompilerParams(vmem_limit_bytes=limit * 2**20, **fields),
        name=name,
    )(*inputs)


def shards(object_field, probes, measured):
    weights = tables()
    wz, wy, wx, vx, vy, vz = [jnp.asarray(weights[k]) for k in range(6)]
    vmem, dma, regular = pltpu.VMEM, pltpu.SemaphoreType.DMA, pltpu.SemaphoreType.REGULAR
    prb = probes[0]
    tiles = (512, 8, H)
    slab = (2, 4, N, N)
    send, own = call(
        transform_zy, "transform_zy", None, tuple(
            pltpu.with_memory_space_constraint(a, pltpu.HBM) for a in (object_field, prb, measured, wz, wy)
        ), (tiles, (N, N)),
        [
            vmem(slab, BF16), vmem(slab, BF16), vmem((N, 4, N), F32), vmem(wz.shape, BF16), vmem(wy.shape, BF16),
            dma((4,)), dma((4,)), dma((6,)),
        ],
        space=pl.ANY,
    )
    (ret,) = call(
        exchange, "exchange", 0, (send, own, wx, vx), (tiles,),
        [vmem(tiles, F32), regular, regular, dma, dma, dma, dma, dma],
    )
    (gradient,) = call(
        update, "update", 1, (object_field, prb, ret, vy, vz), ((2, 4, 32, N),),
        [
            vmem((2, 4, 4, 2, 32, N), F32),
            vmem((4, 4, 2, 32, N), F32),
            vmem((4, 4, 2, 32, N), F32),
            vmem((4, 2, 32, N), F32),
            vmem((4, 2, 2, 32, N), F32),
            dma((4,)), dma((4,)), dma((4, 2)), dma((4, 2)), dma((4, 2)), dma((4, 2)),
        ],
    )
    return gradient


def solution(mesh):
    return jax.shard_map(
        shards,
        mesh=mesh,
        in_specs=(
            P(None, "pen", None, None),
            P("mode", None, "pen", None, None),
            P(None, "pen", None),
        ),
        out_specs=P(None, "pen", "mode", None),
        check_vma=False,
    )
```

```python
import functools
import math

import jax
import jax.numpy as jnp
import ml_dtypes
import numpy as np
from jax import lax
from jax.experimental import pallas as pl
from jax.experimental.pallas import tpu as pltpu
from jax.sharding import PartitionSpec as P

DAMP = 0.1
N = 256
H = N // 2
F32 = jnp.float32
BF16 = jnp.bfloat16
MESH = pl.DeviceIdType.MESH


def forward_matrix(parity):
    freq = 2 * np.arange(H) + parity
    angle = 2.0 * math.pi / N * ((freq[:, None] * np.arange(H)[None, :]) % N)
    cosine, sine = np.cos(angle) / math.sqrt(N), np.sin(angle) / math.sqrt(N)
    return np.block([[cosine, sine], [-sine, cosine]])


def inverse_matrix(parity):
    return forward_matrix(parity).T


def split(matrix):
    high = matrix.astype(ml_dtypes.bfloat16)
    low = (matrix - high.astype(np.float64)).astype(ml_dtypes.bfloat16)
    return np.stack([high, low])


def tables():
    slab, part, row = np.meshgrid(np.arange(H // 4), np.arange(2), np.arange(4), indexing="ij")
    order = (part * H + slab * 4 + row).reshape(-1)
    sets = []
    for parity in range(2):
        fwd, inv = forward_matrix(parity), inverse_matrix(parity)
        sets.append(
            [split(fwd.T), split(fwd), split(fwd[:, order]), split(inv[order, :]), split(inv), split(inv.T)]
        )
    return np.stack([np.stack([sets[0][k], sets[1][k]]) for k in range(6)])


def halves(value):
    high = value.astype(BF16)
    return high, (value - high.astype(F32)).astype(BF16)


def dot(left, right):
    return jnp.dot(left, right, preferred_element_type=F32)


def table_first(table, value):
    high, low = halves(value)
    return dot(table[0], high) + (dot(table[0], low) + dot(table[1], high))


def table_last(value, table):
    high, low = halves(value)
    return dot(high, table[0]) + (dot(low, table[0]) + dot(high, table[1]))


def place():
    mode, pen = lax.axis_index("mode"), lax.axis_index("pen")
    return dict(
        mode=mode, pen=pen, y_hi=mode // 2, core=mode % 2, y=(mode // 2) * 2 + pen // 32, z=(pen // 4) % 8, x=pen % 4
    )


def chip_at(me, step):
    t = (step * 181) % 256
    x, y, z = (me["x"] + t % 4) % 4, (me["y"] + (t // 4) % 8) % 8, (me["z"] + t // 32) % 8
    return y // 2, (y % 2) * 32 + z * 4 + x


def z_peer(me, step):
    return {"pen": me["pen"] // 32 * 32 + (me["z"] + step) % 8 * 4 + me["x"]}


def xy_peer(me, step):
    other = (me["pen"] // 32 * 4 + me["x"] + step) % 8
    return {"pen": other // 4 * 32 + me["z"] * 4 + other % 4}


def mode_peer(me, step):
    return {"mode": (me["mode"] + step) % 8}


def greet(semaphore, me, *kinds):
    for kind in kinds:
        for step in range(1, 8):
            pl.semaphore_signal(semaphore, inc=1, device_id=kind(me, step), device_id_type=MESH)


def ship(source, target, ssem, rsem, device):
    return pltpu.make_async_remote_copy(
        src_ref=source, dst_ref=target, send_sem=ssem, recv_sem=rsem, device_id=device, device_id_type=MESH
    )


def wait_bytes(ref, sem):
    pltpu.make_async_copy(ref, ref, sem).wait()


def exit_wave(obj, prb, x):
    p_re, p_im = prb[0, x].astype(F32), prb[1, x].astype(F32)
    o_re, o_im = obj[0, x].astype(F32), obj[1, x].astype(F32)
    return p_re, p_im, p_re * o_re - p_im * o_im, p_re * o_im + p_im * o_re


def magnitudes(me, own):
    own = jnp.sqrt(own)
    row, column = (lax.broadcasted_iota(jnp.int32, (N, N), k) for k in range(2))
    evens_first = (column == row % H * 2 + row // H).astype(F32)
    rows = jnp.dot(evens_first, own, precision=lax.Precision.HIGHEST, preferred_element_type=F32)
    row, column = (lax.broadcasted_iota(jnp.int32, (N, H), k) for k in range(2))
    chosen = (row == column * 2 + me["core"]).astype(F32)
    return jnp.dot(rows, chosen, precision=lax.Precision.HIGHEST, preferred_element_type=F32)


def transform_zy(
    obj_in, prb_in, meas_in, wz_in, wy_in, send, own, obj, prb, meas, wz, wy, obj_sem, prb_sem, sem
):
    me = place()

    def obj_row(x):
        return pltpu.make_async_copy(obj_in.at[:, x], obj.at[:, x], obj_sem.at[x])

    def prb_row(x):
        return pltpu.make_async_copy(prb_in.at[:, x], prb.at[:, x], prb_sem.at[x])

    table_z = pltpu.make_async_copy(wz_in, wz, sem.at[0])
    table_y = pltpu.make_async_copy(wy_in, wy, sem.at[1])
    intensities = [
        pltpu.make_async_copy(meas_in.at[pl.ds(64 * k, 64)], meas.at[pl.ds(64 * k, 64)], sem.at[2 + k]) for k in range(4)
    ]
    for x in range(2):
        obj_row(x).start()
        prb_row(x).start()
    table_z.start()
    table_y.start()
    for x in range(2, 4):
        obj_row(x).start()
        prb_row(x).start()
    for k in range(4):
        intensities[k].start()

    for half in range(2):
        for two in range(2):
            lines = []
            for x in (2 * two, 2 * two + 1):
                if half == 0:
                    obj_row(x).wait()
                    prb_row(x).wait()
                _, _, e_re, e_im = exit_wave(obj, prb, x)
                if half == 0:
                    mixed = jnp.concatenate([e_re[:, :H] + e_re[:, H:], e_im[:, :H] + e_im[:, H:]], axis=1)
                else:
                    mixed = jnp.concatenate([e_re[:, :H] - e_re[:, H:], e_im[:, :H] - e_im[:, H:]], axis=1)
                if half == 0 and x == 0:
                    table_z.wait()
                    table_y.wait()
                lines.append(table_last(mixed, wz[half]))
            re = jnp.concatenate([lines[0][:, :H], lines[1][:, :H]], axis=1)
            im = jnp.concatenate([lines[0][:, H:], lines[1][:, H:]], axis=1)
            for parity in range(2):
                if parity == 0:
                    mixed = jnp.concatenate([re[:H] + re[H:], im[:H] + im[H:]], axis=0)
                else:
                    mixed = jnp.concatenate([re[:H] - re[H:], im[:H] - im[H:]], axis=0)
                result = table_first(wy[parity], mixed)
                flat = send.at[pl.ds(half * N, N)].reshape(N * 8, H)
                for c in range(2):
                    for k in range(2):
                        rows = pl.ds(parity * 8 + c * 4 + 2 * two + k, H, stride=16)
                        flat[rows, :] = result[c * H : (c + 1) * H, k * H : (k + 1) * H]
    for k in range(4):
        intensities[k].wait()
    own[...] = meas[:, pl.ds(me["y_hi"], 1), :].reshape(N, N)


def send_half(me, half, source, target, send_sem, recv_sem):
    @pl.loop(1, 256)
    def _(step):
        y_hi, pen = chip_at(me, step)
        mode = y_hi * 2 + half
        ship(source(mode, pen), target, send_sem, recv_sem, {"mode": mode, "pen": pen}).start()


def send_home(me, source, target, send_sem, recv_sem, own_sem):
    sibling = me["y_hi"] * 2 + 1 - me["core"]
    ship(source(sibling, me["pen"]), target, send_sem, recv_sem, {"mode": sibling}).start()
    own = pltpu.make_async_copy(source(me["mode"], me["pen"]), target, own_sem)
    own.start()
    own.wait()


def exchange(
    send, own, wx, vx, ret, recv, lines, planes, send_sem, recv_sem, back_sem, ret_sem, own_sem
):
    me = place()
    barrier = pltpu.get_barrier_semaphore()

    def tile(mode, pen):
        return send.at[mode % 2 * N + 4 * pen + mode // 2]

    landing = recv.at[me["mode"] * 64 + me["pen"]]

    def pass_on(half, by_chip, by_xy, least):
        mode = (me["y_hi"] + by_chip % 4) % 4 * 2 + half
        z, xy = (me["z"] + by_chip // 4) % 8, (me["pen"] // 32 * 4 + me["x"] + by_xy) % 8
        pen = xy // 4 * 32 + z * 4 + xy % 4
        differ = [jnp.where(d, 1, 0) for d in (mode != me["mode"], by_chip // 4 != 0, by_xy != 0)]

        @pl.when(differ[0] + differ[1] + differ[2] >= least)
        def _():
            ship(tile(mode, pen), landing, send_sem, recv_sem, {"mode": mode, "pen": pen}).start()

    greet(barrier, me, mode_peer, z_peer, xy_peer)
    pl.semaphore_wait(barrier, 21)
    greet(lines, me, z_peer)

    @pl.loop(0, 4)
    def _(step):
        pass_on(0, step, 0, 1)

    @pl.when(me["core"] == 0)
    def _():
        @pl.loop(1, 8)
        def _(step):
            pass_on(0, step * 4, 0, 1)
            pass_on(0, 0, step, 1)

    pl.semaphore_wait(lines, 7)
    greet(planes, me, xy_peer)

    @pl.loop(0, 32)
    def _(step):
        pass_on(0, step * 13 % 32, 0, 2)

    pl.semaphore_wait(planes, 7)

    @pl.loop(0, 224)
    def _(step):
        t = step * 93 % 224
        pass_on(0, t % 32, 1 + t // 32, 2)

    @pl.loop(0, 256)
    def _(step):
        t = step * 181 % 256
        pass_on(1, t % 32, t // 32, 1)

    own_tile = pltpu.make_async_copy(tile(me["mode"], me["pen"]), landing, own_sem)
    own_tile.start()
    own_tile.wait()
    root = magnitudes(me, own[...])
    wait_bytes(recv.at[pl.ds(0, 511)], recv_sem)

    def slab(mode):
        return recv.at[pl.ds(64 * mode, 64)].reshape(2 * N, H)

    power = [jnp.zeros((H, H), F32), jnp.zeros((H, H), F32)]
    for two in range(4):
        value = jnp.concatenate([slab(2 * two + k)[...] for k in range(2)], axis=1)
        top, bottom = value[:N], value[N:]
        for parity in range(2):
            result = table_first(wx[parity], top + bottom if parity == 0 else top - bottom)
            for k in range(2):
                slab(2 * two + k)[parity * N : (parity + 1) * N, :] = result[:, k * H : (k + 1) * H]
            square = result * result
            square = square[:H] + square[H:]
            power[parity] = power[parity] + (square[:, :H] + square[:, H:])
    ratio = [root[parity * H : (parity + 1) * H] / jnp.sqrt(power[parity] + DAMP) for parity in range(2)]
    ratio = [jnp.concatenate([r, r], axis=0) for r in ratio]
    ratio = [jnp.concatenate([r, r], axis=1) for r in ratio]

    def home(mode, pen):
        return recv.at[mode * 64 + pen]

    target = ret.at[me["core"] * N + 4 * me["pen"] + me["y_hi"]]
    for half in range(2):
        for two in range(2):
            modes = (4 * two + half, 4 * two + 2 + half)
            parts = []
            for parity in range(2):
                rows = slice(parity * N, (parity + 1) * N)
                value = jnp.concatenate([slab(mode)[rows, :] for mode in modes], axis=1)
                parts.append(table_first(vx[parity], value * ratio[parity]))
            for side in range(2):
                result = parts[0] + parts[1] if side == 0 else parts[0] - parts[1]
                for k in range(2):
                    slab(modes[k])[side * N : (side + 1) * N, :] = result[:, k * H : (k + 1) * H]
        send_half(me, half, home, target, back_sem, ret_sem)
    send_home(me, home, target, back_sem, ret_sem, own_sem)
    wait_bytes(ret.at[pl.ds(0, 511)], ret_sem)
    wait_bytes(ret.at[pl.ds(0, 511)], back_sem)
    wait_bytes(ret.at[pl.ds(0, 511)], send_sem)


def update(
    obj, prb, ret, vy, vz, out, part, pair, total, early, near,
    pair_send, pair_recv, early_send, early_recv, near_send, near_recv,
):
    me = place()
    core, other, y_hi = me["core"], 1 - me["core"], me["y_hi"]
    barrier = pltpu.get_barrier_semaphore()
    ways = (1, 3)

    def chip(d):
        return {"mode": (y_hi + d) % 4 * 2 + core}

    for device in ({"mode": y_hi * 2 + other}, chip(1), chip(3)):
        pl.semaphore_signal(barrier, inc=1, device_id=device, device_id_type=MESH)

    def to_core(x):
        return ship(
            part.at[other, x], pair.at[x], pair_send.at[x], pair_recv.at[x], {"mode": y_hi * 2 + other}
        )

    def early_to(x, way):
        return ship(
            total.at[x, (y_hi + 2) % 4, way], early.at[x, way], early_send.at[x, way], early_recv.at[x, way],
            chip(ways[way]),
        )

    def near_to(x, way):
        return ship(
            total.at[x, (y_hi + ways[way]) % 4], near.at[x, way], near_send.at[x, way], near_recv.at[x, way],
            chip(ways[way]),
        )

    def first(x):
        to_core(x).wait_recv()
        total[x] = part[core, x] + pair[x]
        for way in range(2):
            early_to(x, way).start()

    def second(x):
        for way in range(2):
            early_to(x, way).wait_recv()
            total[x, (y_hi + ways[way]) % 4, way] += early[x, way]
            near_to(x, way).start()

    for two in range(2):
        columns = []
        for half in range(2):
            flat = ret.at[pl.ds(half * N, N)].reshape(N * 8, H)
            pieces = []
            for parity in range(2):
                blocks = [
                    [flat[pl.ds(parity * 8 + c * 4 + 2 * two + k, H, stride=16), :] for k in range(2)]
                    for c in range(2)
                ]
                value = jnp.concatenate([jnp.concatenate(b, axis=1) for b in blocks], axis=0)
                pieces.append(table_first(vy[parity], value))
            columns.append((pieces[0] + pieces[1], pieces[0] - pieces[1]))
        for k in range(2):
            x = 2 * two + k
            lanes = slice(k * H, (k + 1) * H)
            lines = []
            for half in range(2):
                top, bottom = columns[half]
                re = jnp.concatenate([top[:H, lanes], bottom[:H, lanes]], axis=0)
                im = jnp.concatenate([top[H:, lanes], bottom[H:, lanes]], axis=0)
                lines.append(table_last(jnp.concatenate([re, im], axis=1), vz[half]))
            low, high = lines[0] + lines[1], lines[0] - lines[1]
            p_re, p_im, e_re, e_im = exit_wave(obj, prb, x)
            d_re = jnp.concatenate([low[:, :H], high[:, :H]], axis=1) - e_re
            d_im = jnp.concatenate([low[:, H:], high[:, H:]], axis=1) - e_im
            g_re = p_re * d_re + p_im * d_im
            g_im = p_re * d_im - p_im * d_re
            for chunk in range(8):
                rows = slice(32 * chunk, 32 * chunk + 32)
                part[chunk % 2, x, chunk // 2, 0] = g_re[rows]
                part[chunk % 2, x, chunk // 2, 1] = g_im[rows]
            if x == 0:
                pl.semaphore_wait(barrier, 3)
            to_core(x).start()
            if x > 0:
                first(x - 1)
            if x > 1:
                second(x - 2)
    first(3)
    second(2)
    second(3)
    for x in range(4):
        for way in range(2):
            near_to(x, way).wait_recv()
        out[:, x] = total[x, y_hi] + (near[x, 0] + near[x, 1])
    for x in range(4):
        to_core(x).wait_send()
        for way in range(2):
            early_to(x, way).wait_send()
            near_to(x, way).wait_send()


def call(body, name, number, inputs, results, scratch, limit=40, space=pltpu.VMEM):
    fields = dict(collective_id=number, has_side_effects=True) if number is not None else {}
    return pl.pallas_call(
        body,
        out_shape=[jax.ShapeDtypeStruct(shape, F32) for shape in results],
        in_specs=[pl.BlockSpec(memory_space=space)] * len(inputs),
        out_specs=[pl.BlockSpec(memory_space=pltpu.VMEM)] * len(results),
        scratch_shapes=scratch,
        compiler_params=pltpu.CompilerParams(vmem_limit_bytes=limit * 2**20, **fields),
        name=name,
    )(*inputs)


def shards(object_field, probes, measured):
    weights = tables()
    wz, wy, wx, vx, vy, vz = [jnp.asarray(weights[k]) for k in range(6)]
    vmem, dma, regular = pltpu.VMEM, pltpu.SemaphoreType.DMA, pltpu.SemaphoreType.REGULAR
    prb = probes[0]
    tiles = (512, 8, H)
    slab = (2, 4, N, N)
    send, own = call(
        transform_zy, "transform_zy", None, tuple(
            pltpu.with_memory_space_constraint(a, pltpu.HBM) for a in (object_field, prb, measured, wz, wy)
        ), (tiles, (N, N)),
        [
            vmem(slab, BF16), vmem(slab, BF16), vmem((N, 4, N), F32), vmem(wz.shape, BF16), vmem(wy.shape, BF16),
            dma((4,)), dma((4,)), dma((6,)),
        ],
        space=pl.ANY,
    )
    (ret,) = call(
        exchange, "exchange", 0, (send, own, wx, vx), (tiles,),
        [vmem(tiles, F32), regular, regular, dma, dma, dma, dma, dma],
    )
    (gradient,) = call(
        update, "update", 1, (object_field, prb, ret, vy, vz), ((2, 4, 32, N),),
        [
            vmem((2, 4, 4, 2, 32, N), F32),
            vmem((4, 4, 2, 32, N), F32),
            vmem((4, 4, 2, 32, N), F32),
            vmem((4, 2, 32, N), F32),
            vmem((4, 2, 2, 32, N), F32),
            dma((4,)), dma((4,)), dma((4, 2)), dma((4, 2)), dma((4, 2)), dma((4, 2)),
        ],
    )
    return gradient


def solution(mesh):
    return jax.shard_map(
        shards,
        mesh=mesh,
        in_specs=(
            P(None, "pen", None, None),
            P("mode", None, "pen", None, None),
            P(None, "pen", None),
        ),
        out_specs=P(None, "pen", "mode", None),
        check_vma=False,
    )
```
